32 devices in a mesh: wide: 16 (over z, y, x), narrow: 2 (over core).
Axes of the slice: x: 2, y: 2, z: 4, core: 2. Of those that a mesh axis runs over, the one named last changes fastest.
Arguments:
- tokens: bfloat16 [12288, 2048], P('wide', 'narrow'), may hold values from -6 to 6
- norm_gain: float32 [2048], replicated, may hold values from 0.1 to 1.9
- qkv_weight: bfloat16 [2048, 3, 2048], P('wide', None, 'narrow'), may hold values from -0.125 to 0.125
- out_weight: bfloat16 [2048, 2048], P('wide', 'narrow'), may hold values from -0.25 to 0.25
- cache_pool: bfloat16 [384, 128, 2, 2048], P('wide', None, None, 'narrow'), may hold values from -400 to 400, as said below
- prefix_pool: bfloat16 [2048, 2, 2048], P('wide', None, 'narrow'), may hold values from -6 to 6
- page_table: int32 [16, 24], P('wide'), may hold values from 0 to 23, each once within a row
- cache_len: int32 [16], P('wide'), may hold values from 512 to 3072
- group_ids: int32 [16], P('wide'), may hold values from 0 to 7, as said below
- group_pages: int32 [16], replicated, may hold values from 0 to 15, each once
Outputs:
- branch_out: bfloat16 [12288, 2048], P('wide', 'narrow')
- new_pages: bfloat16 [12288, 2, 2048], P('wide', None, 'narrow')
The draws below stay inside these ranges and needn't reach their ends.
Inputs may be any that keep to these rules, and one draw needn't show every extreme that they name: `page_table`: each row is a permutation of the 24 pages of that request. `group_ids`: each group has 2 requests. `group_pages`: a permutation of the prefix pool's pages. `cache_pool`: keys are stored already rotated.
All inputs are finite; a program needn't handle non-finite values.
Results may differ from the reference program's by a relative error of at most 0.0095.
The reference program's roundings to bfloat16 on the way count: a program that leaves them out, or rounds other values in their place, can miss the bound.
Values may be sent and summed in bfloat16 or wider, within the bound.
A program may use at most 128 MiB of HBM per device.

```python
import jax
import jax.numpy as jnp
from jax import lax

D = 2048
HEADS = 32
HEAD_DIM = 64
ROT = 16
SPAN = 768
PAGE = 128
SLOTS = 24
GROUPS = 8
PPAGES = 2
REQS = 16
TOKENS = 12288
PREF_TOK = 2048


def draw_cache_pool(key, part):
    normal_part = jax.random.normal(jax.random.fold_in(key, 11), (REQS, SLOTS, PAGE, 2, D), jnp.float32)
    normal_part = jnp.clip(normal_part, -6.0, 6.0)
    return normal_part.reshape(REQS * SLOTS, PAGE, 2, D).astype(jnp.bfloat16)


def draw_cache_len(key, part):
    shortest = 4 * PAGE
    longest = SLOTS * PAGE
    drawn = jax.random.randint(jax.random.fold_in(key, 21), (REQS,), 0, 1001)
    cubed = drawn * drawn // 1000 * drawn // 1000
    lengths = shortest + cubed * (longest - shortest) // 1000
    chosen_one = jax.random.randint(jax.random.fold_in(key, 22), (), 0, REQS)
    return jnp.where(jnp.arange(REQS) == chosen_one, longest, lengths).astype(jnp.int32)


def draw_group_ids(key, part):
    shuffled = jax.random.permutation(jax.random.fold_in(key, 31), REQS)
    return (shuffled % GROUPS).astype(jnp.int32)


def block_scale(own_key, extent, pieces, least, high):
    def one(axis_at, blocks):
        heights = jax.random.uniform(jax.random.fold_in(jax.random.fold_in(own_key, 6), axis_at), (blocks,), jnp.float32, least / len(pieces), high / len(pieces))
        return jnp.repeat(jnp.exp(heights), extent[axis_at] // blocks).reshape((-1,) + (1,) * (len(extent) - axis_at - 1))

    factor_of = one(*pieces[0])
    for cut in pieces[1:]:
        factor_of = factor_of * one(*cut)
    return factor_of


def gaussian(own_key, shape, spread, bound, cuts=(), kind=jnp.bfloat16):
    array = spread * jax.random.normal(own_key, shape, jnp.float32)
    if cuts:
        array = array * block_scale(own_key, shape, cuts, -0.22, 0.18)
    return jnp.clip(array, -bound, bound).astype(kind)


def setup_inputs(seed: int = 0) -> dict:
    streams_of = jax.random.split(jax.random.key(seed), 11)
    tokens = gaussian(streams_of[0], (TOKENS, D), 1.0, 6.0, ((0, 16), (1, 2)))
    norm_gain = jnp.clip(1.0 + 0.18 * jax.random.normal(streams_of[1], (D,), jnp.float32), 0.1, 1.9)
    qkv_weight = gaussian(streams_of[2], (D, 3, D), D ** -0.5, 0.125, ((0, 16), (2, 2)))
    out_weight = gaussian(streams_of[3], (D, D), (D // 4) ** -0.5, 0.25, ((0, 16), (1, 2)))
    cache_pool = draw_cache_pool(jax.random.fold_in(streams_of[10], 71), 0)
    prefix_pool = gaussian(streams_of[5], (PREF_TOK, 2, D), 1.0, 6.0, ((0, 16), (2, 2)))
    page_table = jax.vmap(lambda own: jax.random.permutation(own, SLOTS))(jax.random.split(streams_of[6], REQS)).reshape((REQS, SLOTS)).astype(jnp.int32)
    cache_len = draw_cache_len(jax.random.fold_in(streams_of[10], 71), 0)
    group_ids = draw_group_ids(jax.random.fold_in(streams_of[10], 71), 0)
    group_pages = jax.random.permutation(streams_of[9], GROUPS * PPAGES).astype(jnp.int32)
    return {"tokens": tokens, "norm_gain": norm_gain, "qkv_weight": qkv_weight, "out_weight": out_weight, "cache_pool": cache_pool, "prefix_pool": prefix_pool, "page_table": page_table, "cache_len": cache_len, "group_ids": group_ids, "group_pages": group_pages}


NEGATIVE = -1e+30

def rotary(vectors, positions):
    half_rot = ROT // 2
    frequency = 10000.0 ** (-(jnp.arange(half_rot, dtype=jnp.float32) * 2.0 / ROT))
    angles = positions.astype(jnp.float32)[:, None] * frequency[None, :]
    cos_part = jnp.concatenate([jnp.cos(angles), jnp.cos(angles)], axis=1)[:, None, :]
    sine_part = jnp.concatenate([jnp.sin(angles), jnp.sin(angles)], axis=1)[:, None, :]
    rotated_in = vectors[..., :ROT]
    turned = jnp.concatenate([-rotated_in[..., half_rot:], rotated_in[..., :half_rot]], axis=-1)
    return jnp.concatenate([rotated_in * cos_part + turned * sine_part, vectors[..., ROT:]], axis=-1)

def reference(tokens, norm_gain, qkv_weight, out_weight, cache_pool, prefix_pool, page_table, cache_len, group_ids, group_pages):
    token_count = tokens.shape[0]
    widened = tokens.astype(jnp.float32)
    row_mean = lax.optimization_barrier(jnp.mean(widened, axis=1, keepdims=True))
    centered = widened - row_mean
    variance = lax.optimization_barrier(jnp.mean(centered * centered, axis=1, keepdims=True))
    normed = (centered * lax.rsqrt(variance + 1e-05) * norm_gain.astype(jnp.float32)).astype(jnp.bfloat16)
    projected = jnp.dot(normed, qkv_weight.reshape(D, 3 * D), preferred_element_type=jnp.float32)
    projected = projected.reshape(token_count, 3, HEADS, HEAD_DIM)
    offset = jnp.arange(SPAN, dtype=jnp.int32)
    positions = (PPAGES * PAGE + cache_len[:, None] + offset[None, :]).reshape(token_count).astype(jnp.int32)
    queries = lax.optimization_barrier(rotary(projected[:, 0], positions).astype(jnp.bfloat16))
    keys = lax.optimization_barrier(rotary(projected[:, 1], positions).astype(jnp.bfloat16))
    values = lax.optimization_barrier(projected[:, 2].astype(jnp.bfloat16))
    new_pages = jnp.stack([keys.reshape(token_count, D), values.reshape(token_count, D)], axis=1)
    pool_pages = cache_pool.reshape(REQS, SLOTS, PAGE, 2, HEADS, HEAD_DIM)
    prefix_pages = prefix_pool.reshape(GROUPS * PPAGES, PAGE, 2, HEADS, HEAD_DIM)
    causal = offset[:, None] >= offset[None, :]
    cache_index = jnp.arange(SLOTS * PAGE, dtype=jnp.int32)

    def one_request(items):
        own_queries, own_keys, own_values, own_pool, page_list, length, my_group = items
        cached = jnp.take(own_pool, page_list, axis=0).reshape(SLOTS * PAGE, 2, HEADS, HEAD_DIM)
        chosen = lax.dynamic_slice_in_dim(group_pages, (my_group * PPAGES).astype(jnp.int32), PPAGES)
        shared = jnp.take(prefix_pages, chosen, axis=0).reshape(PPAGES * PAGE, 2, HEADS, HEAD_DIM)
        all_keys = jnp.concatenate([shared[:, 0], cached[:, 0], own_keys], axis=0).astype(jnp.float32)
        all_values = jnp.concatenate([shared[:, 1], cached[:, 1], own_values], axis=0).astype(jnp.float32)
        key_valid = jnp.concatenate([jnp.ones((SPAN, PPAGES * PAGE), dtype=bool), jnp.broadcast_to((cache_index < length)[None, :], (SPAN, SLOTS * PAGE)), causal], axis=1)
        scores = jnp.einsum('qhd,khd->hqk', own_queries.astype(jnp.float32), all_keys) * 0.125
        scores = jnp.where(key_valid[None], scores, NEGATIVE)
        row_max = lax.optimization_barrier(jnp.max(scores, axis=2, keepdims=True))
        expo = jnp.where(key_valid[None], jnp.exp(scores - row_max), 0.0)
        denominator = lax.optimization_barrier(jnp.sum(expo, axis=2))
        probs = lax.optimization_barrier(expo.astype(jnp.bfloat16))
        weighted = jnp.einsum('hqk,khd->qhd', probs.astype(jnp.float32), all_values)
        return (weighted / jnp.transpose(denominator)[:, :, None]).astype(jnp.bfloat16)
    attended = lax.map(one_request, (queries.reshape(REQS, SPAN, HEADS, HEAD_DIM), keys.reshape(REQS, SPAN, HEADS, HEAD_DIM), values.reshape(REQS, SPAN, HEADS, HEAD_DIM), pool_pages, page_table, cache_len, group_ids))
    attended = attended.reshape(token_count, D)
    branch_out = jnp.dot(attended, out_weight, preferred_element_type=jnp.float32).astype(jnp.bfloat16)
    return (branch_out, new_pages)
```

```python
import functools

import jax
import jax.numpy as jnp
from jax import lax
from jax.experimental import pallas as pl
from jax.experimental.pallas import tpu as pltpu
from jax.sharding import PartitionSpec as P

HEAD_DIM = 64
ROT = 16
PAGE = 128
PPAGES = 2
LANES = 128
NEGATIVE = -1e30
LOG2E = 1.4426950408889634
VMEM = 44 * 1024 * 1024


def flip(value, axis, size, bit):
    pairs = [(i, i ^ (1 << bit)) for i in range(size)]
    return lax.ppermute(value, axis, pairs)


def after(value, *earlier):
    return lax.optimization_barrier((value,) + earlier)[0]


class Gather:
    def __init__(self, me, size, shard_rows):
        self.me, self.size = me, size
        bits = size.bit_length() - 1
        self.low = max(0, (LANES // shard_rows).bit_length() - 1)
        order = list(range(bits))
        if self.low == 0:
            order = order[2:][::-1] + order[:2]
        self.base, self.u, self.v = order[:-2], order[-2], order[-1]
        self.order = order

    def base_stages(self, piece):
        for k, bit in enumerate(self.base):
            got = flip(piece, "wide", self.size, bit)
            if k < self.low:
                upper = (self.me >> bit) & 1
                piece = jnp.where(
                    upper == 1,
                    jnp.concatenate([got, piece], axis=0),
                    jnp.concatenate([piece, got], axis=0),
                )
            else:
                piece = jnp.concatenate([piece, got], axis=0)
        return piece

    def last_stages(self, piece, swapped):
        first, second = (self.v, self.u) if swapped else (self.u, self.v)
        piece = jnp.concatenate([piece, flip(piece, "wide", self.size, first)], axis=0)
        return piece, flip(piece, "wide", self.size, second)

    def blocks(self):
        relative = [0]
        for bit in self.order[self.low :]:
            relative = relative + [r ^ (1 << (bit - self.low)) for r in relative]
        return jnp.asarray(relative, jnp.int32) ^ (self.me >> self.low)


def norm_body(src_ref, blk_ref, x_ref, gain_ref, out_ref):
    wide_x = x_ref[...].astype(jnp.float32)
    mean = jnp.mean(wide_x, axis=1, keepdims=True)
    centered = wide_x - mean
    inv = lax.rsqrt(jnp.mean(centered * centered, axis=1, keepdims=True) + 1e-05)
    for j in range(x_ref.shape[1] // LANES):
        src = pl.multiple_of(src_ref[j] * LANES, LANES)
        blk = pl.multiple_of(blk_ref[j] * LANES, LANES)
        part = x_ref[:, pl.ds(src, LANES)].astype(jnp.float32) - mean
        out_ref[:, j * LANES : (j + 1) * LANES] = (
            part * inv * gain_ref[:, pl.ds(blk, LANES)]
        ).astype(jnp.bfloat16)


def norm_permute(tokens, gain, src, blk):
    rows, width = tokens.shape
    tile = 256
    return pl.pallas_call(
        norm_body,
        grid_spec=pltpu.PrefetchScalarGridSpec(
            num_scalar_prefetch=2,
            grid=(rows // tile,),
            in_specs=[
                pl.BlockSpec((tile, width), lambda i, s, b: (i, 0)),
                pl.BlockSpec((1, width), lambda i, s, b: (0, 0)),
            ],
            out_specs=pl.BlockSpec((tile, width), lambda i, s, b: (i, 0)),
        ),
        out_shape=jax.ShapeDtypeStruct((rows, width), jnp.bfloat16),
        compiler_params=pltpu.CompilerParams(vmem_limit_bytes=VMEM),
        cost_estimate=pl.CostEstimate(
            flops=10 * rows * width, bytes_accessed=4 * rows * width, transcendentals=0
        ),
    )(src, blk, tokens, gain.reshape(1, width))


def split_dot(x, p_ref, r_ref, swapped):
    quarter = p_ref.shape[0] // 2
    groups = (0, 2, 1, 3) if swapped else (0, 1, 2, 3)

    def one(at, w):
        return jnp.dot(
            x(groups[at] * quarter, quarter), w, preferred_element_type=jnp.float32
        )

    return (
        one(0, p_ref[:quarter]) + one(1, p_ref[quarter:])
    ) + (one(2, r_ref[:quarter]) + one(3, r_ref[quarter:]))


def project_body(swapped, rotate, scale, x_ref, p_ref, r_ref, c_ref, s_ref, t_ref, *outs):
    total = split_dot(lambda at, n: x_ref[:, at : at + n], p_ref, r_ref, swapped)
    parts = []
    for j in range(total.shape[1] // LANES):
        part = total[:, j * LANES : (j + 1) * LANES]
        if rotate:
            part = (
                part * c_ref[...]
                + pltpu.roll(part, LANES - ROT // 2, 1) * s_ref[...]
                + pltpu.roll(part, ROT // 2, 1) * t_ref[...]
            )
        part = part.astype(jnp.bfloat16)
        if scale:
            part = part * jnp.bfloat16(0.125)
        outs[0][:, j * LANES : (j + 1) * LANES] = part


def project(x, pieces, tables, swapped, rotate, scale):
    rows, depth = x.shape
    half, columns = pieces[0].shape
    tile = min(256, columns)
    whole = lambda i: (0, 0)
    col = lambda i: (0, i)
    return pl.pallas_call(
        functools.partial(project_body, swapped, rotate, scale),
        grid=(columns // tile,),
        in_specs=[
            pl.BlockSpec((rows, depth), whole),
            pl.BlockSpec((half, tile), col),
            pl.BlockSpec((half, tile), col),
        ]
        + [pl.BlockSpec((rows, LANES), whole)] * 3,
        out_specs=pl.BlockSpec((rows, tile), col),
        out_shape=jax.ShapeDtypeStruct((rows, columns), jnp.bfloat16),
        compiler_params=pltpu.CompilerParams(vmem_limit_bytes=VMEM),
        cost_estimate=pl.CostEstimate(
            flops=2 * rows * depth * columns,
            bytes_accessed=2 * (rows * depth + depth * columns + rows * columns),
            transcendentals=0,
        ),
    )(x, *pieces, *tables)


def head_of(pair, head):
    lane = lax.broadcasted_iota(jnp.int32, pair.shape, 1)
    mine = (lane >= HEAD_DIM) if head else (lane < HEAD_DIM)
    return jnp.where(mine, pair, jnp.zeros_like(pair))


def scores_of(q, k):
    return lax.dot_general(q, k, (((1,), (1,)), ((), ())), preferred_element_type=jnp.float32)


def soft(q_ref, k, v, bias, valid):
    ones = jnp.ones_like(v)
    v_ones = jnp.concatenate([v, ones], axis=1)
    rows = q_ref.shape[0]
    found = []
    for head in range(2):
        s = scores_of(head_of(q_ref[...], head), k)
        if bias is not None:
            s = s + bias
        if valid is not None:
            s = jnp.where(valid, s, NEGATIVE)
        m = jnp.max(s, axis=1, keepdims=True)
        p = jnp.exp2((s - m) * LOG2E).astype(jnp.bfloat16)
        o = jnp.dot(p, v_ones, preferred_element_type=jnp.float32)
        found.append((o[:, :LANES], o[:, LANES:], jnp.broadcast_to(m, (rows, LANES))))
    lane = lax.broadcasted_iota(jnp.int32, (rows, LANES), 1) < HEAD_DIM
    return [jnp.where(lane, a, b) for a, b in zip(*found)]


def cache_body(q_ref, k_ref, v_ref, bias_ref, o_ref, l_ref, m_ref):
    o, l, m = soft(q_ref, k_ref[...], v_ref[...], bias_ref[...], None)
    o_ref[...] = o
    l_ref[...] = l
    m_ref[...] = m


def cache_attention(q, k, v, bias, q_at, kv_at, pairs):
    rows = q.shape[0]
    keys = k.shape[0]
    tile = 256
    shape = jax.ShapeDtypeStruct((rows, pairs * LANES), jnp.float32)
    out = pl.BlockSpec((tile, LANES), lambda h, i: (i, h))
    kv = pl.BlockSpec((keys, LANES), lambda h, i: (0, h + kv_at))
    return pl.pallas_call(
        cache_body,
        grid=(pairs, rows // tile),
        in_specs=[
            pl.BlockSpec((tile, LANES), lambda h, i: (i, h + q_at)),
            kv,
            kv,
            pl.BlockSpec((1, keys), lambda h, i: (0, 0)),
        ],
        out_specs=[out] * 3,
        out_shape=[shape] * 3,
        compiler_params=pltpu.CompilerParams(vmem_limit_bytes=VMEM),
        cost_estimate=pl.CostEstimate(
            flops=pairs * 2 * rows * keys * 256 * 4,
            bytes_accessed=pairs * (keys * 512 + rows * 1800),
            transcendentals=pairs * 2 * rows * keys,
        ),
    )(q, k, v, bias)


def own_body(q_ref, kn_ref, vn_ref, kp_ref, vp_ref, o_ref, l_ref, m_ref, out_ref):
    rows = q_ref.shape[0]
    shared = kp_ref.shape[0]
    keys = shared + kn_ref.shape[0]
    k = jnp.concatenate([kp_ref[...], kn_ref[...]], axis=0)
    v = jnp.concatenate([vp_ref[...], vn_ref[...]], axis=0)
    query = pl.program_id(1) * rows + lax.broadcasted_iota(jnp.int32, (rows, keys), 0)
    key = lax.broadcasted_iota(jnp.int32, (rows, keys), 1) - shared
    o2, l2, m2 = soft(q_ref, k, v, None, key <= query)
    m1 = m_ref[...]
    m = jnp.maximum(m1, m2)
    f1 = jnp.exp2((m1 - m) * LOG2E)
    f2 = jnp.exp2((m2 - m) * LOG2E)
    out_ref[...] = (
        (o_ref[...] * f1 + o2 * f2) / (l_ref[...] * f1 + l2 * f2)
    ).astype(jnp.bfloat16)


def own_attention(q, kn, vn, kp, vp, state, q_at, kv_at):
    rows = q.shape[0]
    shared = kp.shape[0]
    pairs = state[0].shape[1] // LANES
    tile = 256
    here = pl.BlockSpec((tile, LANES), lambda h, i: (i, h))
    new = pl.BlockSpec((rows, LANES), lambda h, i: (0, h + q_at))
    pre = pl.BlockSpec((shared, LANES), lambda h, i: (0, h + kv_at))
    return pl.pallas_call(
        own_body,
        grid=(pairs, rows // tile),
        in_specs=[
            pl.BlockSpec((tile, LANES), lambda h, i: (i, h + q_at)),
            new,
            new,
            pre,
            pre,
            here,
            here,
            here,
        ],
        out_specs=here,
        out_shape=jax.ShapeDtypeStruct((rows, pairs * LANES), jnp.bfloat16),
        compiler_params=pltpu.CompilerParams(vmem_limit_bytes=VMEM),
        cost_estimate=pl.CostEstimate(
            flops=pairs * 2 * rows * (shared + rows) * 256 * 4,
            bytes_accessed=pairs * rows * 2800,
            transcendentals=pairs * 2 * rows * (shared + rows),
        ),
    )(q, kn, vn, kp, vp, *state)


def output_body(src_ref, x_ref, pa_ref, ra_ref, pb_ref, rb_ref, out_ref, turned):
    for j in range(x_ref.shape[1] // LANES):
        src = pl.multiple_of(src_ref[j] * LANES, LANES)
        turned[:, j * LANES : (j + 1) * LANES] = x_ref[:, pl.ds(src, LANES)]
    half = pa_ref.shape[1]
    x = lambda at, n: turned[:, at : at + n]
    out_ref[:, :half] = split_dot(x, pa_ref, ra_ref, False).astype(jnp.bfloat16)
    out_ref[:, half:] = split_dot(x, pb_ref, rb_ref, True).astype(jnp.bfloat16)


def output(x, src, pieces_a, pieces_b):
    rows, depth = x.shape
    half, columns = pieces_a[0].shape
    tile = 256
    weight = pl.BlockSpec((half, columns), lambda i, s: (0, 0))
    return pl.pallas_call(
        output_body,
        grid_spec=pltpu.PrefetchScalarGridSpec(
            num_scalar_prefetch=1,
            grid=(rows // tile,),
            in_specs=[pl.BlockSpec((tile, depth), lambda i, s: (i, 0))] + [weight] * 4,
            out_specs=pl.BlockSpec((tile, 2 * columns), lambda i, s: (i, 0)),
            scratch_shapes=[pltpu.VMEM((tile, depth), jnp.bfloat16)],
        ),
        out_shape=jax.ShapeDtypeStruct((rows, 2 * columns), jnp.bfloat16),
        compiler_params=pltpu.CompilerParams(vmem_limit_bytes=VMEM),
        cost_estimate=pl.CostEstimate(
            flops=4 * rows * depth * columns,
            bytes_accessed=2 * depth * (rows + 2 * columns),
            transcendentals=0,
        ),
    )(src, x, *pieces_a, *pieces_b)


def rotary_tables(positions):
    half_rot = ROT // 2
    frequency = 10000.0 ** (-(jnp.arange(half_rot, dtype=jnp.float32) * 2.0 / ROT))
    angles = positions.astype(jnp.float32)[:, None] * frequency[None, :]
    cos, sin = jnp.cos(angles), jnp.sin(angles)
    rows = positions.shape[0]
    rest = jnp.zeros((rows, HEAD_DIM - ROT), jnp.float32)
    none = jnp.zeros_like(sin)
    tables = (
        jnp.concatenate([cos, cos, rest + 1.0], axis=1),
        jnp.concatenate([-sin, none, rest], axis=1),
        jnp.concatenate([none, sin, rest], axis=1),
    )
    return [jnp.concatenate([t, t], axis=1) for t in tables]


def narrow_gather(value, size):
    bit = 0
    while (1 << bit) < size:
        value = jnp.concatenate([value, flip(value, "narrow", size, bit)], axis=1)
        bit += 1
    return value


def local(
    wide,
    narrow,
    tokens,
    norm_gain,
    qkv_weight,
    out_weight,
    cache_pool,
    prefix_pool,
    page_table,
    cache_len,
    group_ids,
    group_pages,
):
    rows = tokens.shape[0]
    width = qkv_weight.shape[2]
    half = width // 2
    me = lax.axis_index("wide")
    me_narrow = lax.axis_index("narrow")
    shard = qkv_weight.shape[0]
    gather = Gather(me, wide, shard)
    per_narrow = width // LANES
    blocks = gather.blocks()
    places = ((blocks // per_narrow) ^ me_narrow) * per_narrow + blocks % per_narrow

    all_tokens = narrow_gather(tokens, narrow)

    def halves(w):
        return w[:, :half], w[:, half:]

    pieces = {}
    earlier = ()
    parts = [("q", qkv_weight[:, 0]), ("k", qkv_weight[:, 1]), ("v", qkv_weight[:, 2]), ("o", out_weight)]
    prefix_start = None
    for name, w in parts:
        wa, wb = halves(after(w, *earlier))
        ba, bb = gather.base_stages(wa), gather.base_stages(wb)
        pieces[name] = (gather.last_stages(ba, False), gather.last_stages(bb, True))
        earlier = (ba, bb)
        if name == "k":
            prefix_start = (ba, bb)

    shard_rows = prefix_pool.shape[0]
    per_page = PAGE // shard_rows
    page_ids = lax.dynamic_slice_in_dim(group_pages, group_ids[0] * PPAGES, PPAGES)
    need = (page_ids[:, None] * per_page + jnp.arange(per_page, dtype=jnp.int32)[None, :]).reshape(-1)
    need_there = flip(need, "wide", wide, gather.v)
    held = after(prefix_pool, *prefix_start)
    for bit in gather.order[:-1]:
        held = jnp.concatenate([held, flip(held, "wide", wide, bit)], axis=0)

    def pick(ids):
        relative = ids ^ me
        at = jnp.zeros_like(ids)
        for k, bit in enumerate(gather.order[:-1]):
            at = at + (((relative >> bit) & 1) << k)
        return jnp.concatenate(
            [
                lax.dynamic_slice_in_dim(held, at[i] * shard_rows, shard_rows)
                for i in range(ids.shape[0])
            ],
            axis=0,
        )

    sent = flip(pick(need_there), "wide", wide, gather.v)
    from_there = jnp.repeat(((need ^ me) >> gather.v) & 1, shard_rows)
    prefix = jnp.where(from_there[:, None, None] == 1, sent, pick(need))
    prefix_k, prefix_v = prefix[:, 0], prefix[:, 1]

    x = norm_permute(all_tokens, norm_gain, places, blocks)
    length = cache_len[0]
    positions = PPAGES * PAGE + length + jnp.arange(rows, dtype=jnp.int32)
    tables = rotary_tables(positions)
    slots = page_table.shape[1]
    slot_of = jnp.argsort(page_table[0]).astype(jnp.int32)
    token_at = slot_of[:, None] * PAGE + jnp.arange(PAGE, dtype=jnp.int32)[None, :]
    bias = jnp.where(token_at < length, 0.0, NEGATIVE).astype(jnp.float32).reshape(1, slots * PAGE)
    cache_k = cache_pool[:, :, 0].reshape(slots * PAGE, width)
    cache_v = cache_pool[:, :, 1].reshape(slots * PAGE, width)

    q = [project(x, pieces["q"][s], tables, bool(s), True, True) for s in range(2)]
    pairs = half // LANES
    step = max(1, pairs // 2)
    states = []
    for s in range(2):
        for at in range(0, pairs, step):
            states.append(
                (s, at, cache_attention(q[s], cache_k, cache_v, bias, at, s * pairs + at, step))
            )
    k = [project(x, pieces["k"][s], tables, bool(s), True, False) for s in range(2)]
    v = [project(x, pieces["v"][s], tables, bool(s), False, False) for s in range(2)]
    attended = jnp.concatenate(
        [
            own_attention(q[s], k[s], v[s], prefix_k, prefix_v, state, at, s * pairs + at)
            for s, at, state in states
        ],
        axis=1,
    )
    new_pages = jnp.stack(
        [jnp.concatenate(k, axis=1), jnp.concatenate(v, axis=1)], axis=1
    )
    all_heads = narrow_gather(attended, narrow)
    branch_out = output(all_heads, places, *pieces["o"])
    return (branch_out, new_pages)


def solution(mesh):
    placed = (
        P("wide", "narrow"),
        P(),
        P("wide", None, "narrow"),
        P("wide", "narrow"),
        P("wide", None, None, "narrow"),
        P("wide", None, "narrow"),
        P("wide", None),
        P("wide"),
        P("wide"),
        P(),
    )
    return jax.shard_map(
        functools.partial(local, mesh.shape["wide"], mesh.shape["narrow"]),
        mesh=mesh,
        in_specs=placed,
        out_specs=(P("wide", "narrow"), P("wide", None, "narrow")),
        check_vma=False,
    )
```

```python
import functools

import jax
import jax.numpy as jnp
from jax import lax
from jax.experimental import pallas as pl
from jax.experimental.pallas import tpu as pltpu
from jax.sharding import PartitionSpec as P

HEAD_DIM = 64
ROT = 16
PAGE = 128
PPAGES = 2
LANES = 128
NEGATIVE = -1e30
LOG2E = 1.4426950408889634
VMEM = 44 * 1024 * 1024


def flip(value, axis, size, bit):
    pairs = [(i, i ^ (1 << bit)) for i in range(size)]
    return lax.ppermute(value, axis, pairs)


def after(value, earlier):
    return lax.optimization_barrier((value, earlier))[0]


class Gather:
    def __init__(self, me, size, shard_rows):
        self.me, self.size = me, size
        bits = size.bit_length() - 1
        self.low = max(0, (LANES // shard_rows).bit_length() - 1)
        order = list(range(bits))
        if self.low == 0:
            order = order[2:][::-1] + order[:2]
        self.base, self.u, self.v = order[:-2], order[-2], order[-1]
        self.order = order

    def base_stages(self, piece):
        for k, bit in enumerate(self.base):
            got = flip(piece, "wide", self.size, bit)
            if k < self.low:
                upper = (self.me >> bit) & 1
                piece = jnp.where(
                    upper == 1,
                    jnp.concatenate([got, piece], axis=0),
                    jnp.concatenate([piece, got], axis=0),
                )
            else:
                piece = jnp.concatenate([piece, got], axis=0)
        return piece

    def last_stages(self, piece, swapped):
        first, second = (self.v, self.u) if swapped else (self.u, self.v)
        piece = jnp.concatenate([piece, flip(piece, "wide", self.size, first)], axis=0)
        return piece, flip(piece, "wide", self.size, second)

    def first_stage(self, piece, swapped):
        bit = self.v if swapped else self.u
        return jnp.concatenate([piece, flip(piece, "wide", self.size, bit)], axis=0)

    def second_stage(self, piece, swapped):
        return flip(piece, "wide", self.size, self.u if swapped else self.v)

    def blocks(self):
        relative = [0]
        for bit in self.order[self.low :]:
            relative = relative + [r ^ (1 << (bit - self.low)) for r in relative]
        return jnp.asarray(relative, jnp.int32) ^ (self.me >> self.low)


def norm_body(src_ref, blk_ref, x_ref, gain_ref, out_ref):
    wide_x = x_ref[...].astype(jnp.float32)
    mean = jnp.mean(wide_x, axis=1, keepdims=True)
    centered = wide_x - mean
    inv = lax.rsqrt(jnp.mean(centered * centered, axis=1, keepdims=True) + 1e-05)
    for j in range(x_ref.shape[1] // LANES):
        src = pl.multiple_of(src_ref[j] * LANES, LANES)
        blk = pl.multiple_of(blk_ref[j] * LANES, LANES)
        part = x_ref[:, pl.ds(src, LANES)].astype(jnp.float32) - mean
        out_ref[:, j * LANES : (j + 1) * LANES] = (
            part * inv * gain_ref[:, pl.ds(blk, LANES)]
        ).astype(jnp.bfloat16)


def norm_permute(tokens, gain, src, blk):
    rows, width = tokens.shape
    tile = 256
    return pl.pallas_call(
        norm_body,
        grid_spec=pltpu.PrefetchScalarGridSpec(
            num_scalar_prefetch=2,
            grid=(rows // tile,),
            in_specs=[
                pl.BlockSpec((tile, width), lambda i, s, b: (i, 0)),
                pl.BlockSpec((1, width), lambda i, s, b: (0, 0)),
            ],
            out_specs=pl.BlockSpec((tile, width), lambda i, s, b: (i, 0)),
        ),
        out_shape=jax.ShapeDtypeStruct((rows, width), jnp.bfloat16),
        compiler_params=pltpu.CompilerParams(vmem_limit_bytes=VMEM),
        cost_estimate=pl.CostEstimate(
            flops=10 * rows * width, bytes_accessed=4 * rows * width, transcendentals=0
        ),
    )(src, blk, tokens, gain.reshape(1, width))


def split_dot(x, p_ref, r_ref, swapped):
    quarter = p_ref.shape[0] // 2
    groups = (0, 2, 1, 3) if swapped else (0, 1, 2, 3)

    def one(at, w):
        return jnp.dot(
            x(groups[at] * quarter, quarter), w, preferred_element_type=jnp.float32
        )

    return (
        one(0, p_ref[:quarter]) + one(1, p_ref[quarter:])
    ) + (one(2, r_ref[:quarter]) + one(3, r_ref[quarter:]))


def project_body(swapped, rotate, scale, x_ref, p_ref, r_ref, c_ref, s_ref, t_ref, *outs):
    total = split_dot(lambda at, n: x_ref[:, at : at + n], p_ref, r_ref, swapped)
    parts = []
    for j in range(total.shape[1] // LANES):
        part = total[:, j * LANES : (j + 1) * LANES]
        if rotate:
            part = (
                part * c_ref[...]
                + pltpu.roll(part, LANES - ROT // 2, 1) * s_ref[...]
                + pltpu.roll(part, ROT // 2, 1) * t_ref[...]
            )
        part = part.astype(jnp.bfloat16)
        if scale:
            part = part * jnp.bfloat16(0.125)
        outs[0][:, j * LANES : (j + 1) * LANES] = part


def project(x, pieces, tables, swapped, rotate, scale):
    rows, depth = x.shape
    half, columns = pieces[0].shape
    tile = min(256, columns)
    whole = lambda i: (0, 0)
    col = lambda i: (0, i)
    return pl.pallas_call(
        functools.partial(project_body, swapped, rotate, scale),
        grid=(columns // tile,),
        in_specs=[
            pl.BlockSpec((rows, depth), whole),
            pl.BlockSpec((half, tile), col),
            pl.BlockSpec((half, tile), col),
        ]
        + [pl.BlockSpec((rows, LANES), whole)] * 3,
        out_specs=pl.BlockSpec((rows, tile), col),
        out_shape=jax.ShapeDtypeStruct((rows, columns), jnp.bfloat16),
        compiler_params=pltpu.CompilerParams(vmem_limit_bytes=VMEM),
        cost_estimate=pl.CostEstimate(
            flops=2 * rows * depth * columns,
            bytes_accessed=2 * (rows * depth + depth * columns + rows * columns),
            transcendentals=0,
        ),
    )(x, *pieces, *tables)


def head_of(pair, head):
    lane = lax.broadcasted_iota(jnp.int32, pair.shape, 1)
    mine = (lane >= HEAD_DIM) if head else (lane < HEAD_DIM)
    return jnp.where(mine, pair, jnp.zeros_like(pair))


def scores_of(q, k):
    return lax.dot_general(q, k, (((1,), (1,)), ((), ())), preferred_element_type=jnp.float32)


def soft(q_ref, k, v, bias, valid):
    ones = jnp.ones_like(v)
    v_ones = jnp.concatenate([v, ones], axis=1)
    rows = q_ref.shape[0]
    found = []
    for head in range(2):
        s = scores_of(head_of(q_ref[...], head), k)
        if bias is not None:
            s = s + bias
        if valid is not None:
            s = jnp.where(valid, s, NEGATIVE)
        m = jnp.max(s, axis=1, keepdims=True)
        p = jnp.exp2((s - m) * LOG2E).astype(jnp.bfloat16)
        o = jnp.dot(p, v_ones, preferred_element_type=jnp.float32)
        found.append((o[:, :LANES], o[:, LANES:], jnp.broadcast_to(m, (rows, LANES))))
    lane = lax.broadcasted_iota(jnp.int32, (rows, LANES), 1) < HEAD_DIM
    return [jnp.where(lane, a, b) for a, b in zip(*found)]


def cache_body(q_ref, k_ref, v_ref, bias_ref, o_ref, l_ref, m_ref):
    o, l, m = soft(q_ref, k_ref[...], v_ref[...], bias_ref[...], None)
    o_ref[...] = o
    l_ref[...] = l
    m_ref[...] = m


def cache_attention(q, k, v, bias, q_at, kv_at, pairs):
    rows = q.shape[0]
    keys = k.shape[0]
    tile = 256
    shape = jax.ShapeDtypeStruct((rows, pairs * LANES), jnp.float32)
    out = pl.BlockSpec((tile, LANES), lambda h, i: (i, h))
    kv = pl.BlockSpec((keys, LANES), lambda h, i: (0, h + kv_at))
    return pl.pallas_call(
        cache_body,
        grid=(pairs, rows // tile),
        in_specs=[
            pl.BlockSpec((tile, LANES), lambda h, i: (i, h + q_at)),
            kv,
            kv,
            pl.BlockSpec((1, keys), lambda h, i: (0, 0)),
        ],
        out_specs=[out] * 3,
        out_shape=[shape] * 3,
        compiler_params=pltpu.CompilerParams(vmem_limit_bytes=VMEM),
        cost_estimate=pl.CostEstimate(flops=1000, bytes_accessed=1000, transcendentals=0),
    )(q, k, v, bias)


def own_body(q_ref, kn_ref, vn_ref, kp_ref, vp_ref, o_ref, l_ref, m_ref, out_ref):
    rows = q_ref.shape[0]
    shared = kp_ref.shape[0]
    keys = shared + kn_ref.shape[0]
    k = jnp.concatenate([kp_ref[...], kn_ref[...]], axis=0)
    v = jnp.concatenate([vp_ref[...], vn_ref[...]], axis=0)
    query = pl.program_id(1) * rows + lax.broadcasted_iota(jnp.int32, (rows, keys), 0)
    key = lax.broadcasted_iota(jnp.int32, (rows, keys), 1) - shared
    o2, l2, m2 = soft(q_ref, k, v, None, key <= query)
    m1 = m_ref[...]
    m = jnp.maximum(m1, m2)
    f1 = jnp.exp2((m1 - m) * LOG2E)
    f2 = jnp.exp2((m2 - m) * LOG2E)
    out_ref[...] = (
        (o_ref[...] * f1 + o2 * f2) / (l_ref[...] * f1 + l2 * f2)
    ).astype(jnp.bfloat16)


def own_attention(q, kn, vn, kp, vp, state, q_at, kv_at):
    rows = q.shape[0]
    shared = kp.shape[0]
    pairs = state[0].shape[1] // LANES
    tile = 256
    here = pl.BlockSpec((tile, LANES), lambda h, i: (i, h))
    new = pl.BlockSpec((rows, LANES), lambda h, i: (0, h + kv_at))
    pre = pl.BlockSpec((shared, LANES), lambda h, i: (0, h + kv_at))
    return pl.pallas_call(
        own_body,
        grid=(pairs, rows // tile),
        in_specs=[
            pl.BlockSpec((tile, LANES), lambda h, i: (i, h + q_at)),
            new,
            new,
            pre,
            pre,
            here,
            here,
            here,
        ],
        out_specs=here,
        out_shape=jax.ShapeDtypeStruct((rows, pairs * LANES), jnp.bfloat16),
        compiler_params=pltpu.CompilerParams(vmem_limit_bytes=VMEM),
        cost_estimate=pl.CostEstimate(flops=1000, bytes_accessed=1000, transcendentals=0),
    )(q, kn, vn, kp, vp, *state)


def output_body(src_ref, x_ref, pa_ref, ra_ref, pb_ref, rb_ref, out_ref, turned):
    for j in range(x_ref.shape[1] // LANES):
        src = pl.multiple_of(src_ref[j] * LANES, LANES)
        turned[:, j * LANES : (j + 1) * LANES] = x_ref[:, pl.ds(src, LANES)]
    half = pa_ref.shape[1]
    x = lambda at, n: turned[:, at : at + n]
    out_ref[:, :half] = split_dot(x, pa_ref, ra_ref, False).astype(jnp.bfloat16)
    out_ref[:, half:] = split_dot(x, pb_ref, rb_ref, True).astype(jnp.bfloat16)


def output(x, src, pieces_a, pieces_b):
    rows, depth = x.shape
    half, columns = pieces_a[0].shape
    tile = 256
    weight = pl.BlockSpec((half, columns), lambda i, s: (0, 0))
    return pl.pallas_call(
        output_body,
        grid_spec=pltpu.PrefetchScalarGridSpec(
            num_scalar_prefetch=1,
            grid=(rows // tile,),
            in_specs=[pl.BlockSpec((tile, depth), lambda i, s: (i, 0))] + [weight] * 4,
            out_specs=pl.BlockSpec((tile, 2 * columns), lambda i, s: (i, 0)),
            scratch_shapes=[pltpu.VMEM((tile, depth), jnp.bfloat16)],
        ),
        out_shape=jax.ShapeDtypeStruct((rows, 2 * columns), jnp.bfloat16),
        compiler_params=pltpu.CompilerParams(vmem_limit_bytes=VMEM),
        cost_estimate=pl.CostEstimate(
            flops=4 * rows * depth * columns,
            bytes_accessed=2 * depth * (rows + 2 * columns),
            transcendentals=0,
        ),
    )(src, x, *pieces_a, *pieces_b)


def rotary_tables(positions):
    half_rot = ROT // 2
    frequency = 10000.0 ** (-(jnp.arange(half_rot, dtype=jnp.float32) * 2.0 / ROT))
    angles = positions.astype(jnp.float32)[:, None] * frequency[None, :]
    cos, sin = jnp.cos(angles), jnp.sin(angles)
    rows = positions.shape[0]
    rest = jnp.zeros((rows, HEAD_DIM - ROT), jnp.float32)
    none = jnp.zeros_like(sin)
    tables = (
        jnp.concatenate([cos, cos, rest + 1.0], axis=1),
        jnp.concatenate([-sin, none, rest], axis=1),
        jnp.concatenate([none, sin, rest], axis=1),
    )
    return [jnp.concatenate([t, t], axis=1) for t in tables]


def narrow_gather(value, size):
    bit = 0
    while (1 << bit) < size:
        value = jnp.concatenate([value, flip(value, "narrow", size, bit)], axis=1)
        bit += 1
    return value


def local(
    wide,
    narrow,
    tokens,
    norm_gain,
    qkv_weight,
    out_weight,
    cache_pool,
    prefix_pool,
    page_table,
    cache_len,
    group_ids,
    group_pages,
):
    rows = tokens.shape[0]
    width = qkv_weight.shape[2]
    half = width // 2
    me = lax.axis_index("wide")
    me_narrow = lax.axis_index("narrow")
    shard = qkv_weight.shape[0]
    gather = Gather(me, wide, shard)
    per_narrow = width // LANES
    blocks = gather.blocks()
    places = ((blocks // per_narrow) ^ me_narrow) * per_narrow + blocks % per_narrow

    all_tokens = narrow_gather(tokens, narrow)

    def halves(w):
        return w[:, :half], w[:, half:]

    qa, qb = halves(qkv_weight[:, 0])
    qa, qb = gather.base_stages(qa), gather.base_stages(qb)
    q_pieces = (gather.last_stages(qa, False), gather.last_stages(qb, True))
    gate = (q_pieces[0][0], q_pieces[1][0])
    later_k, later_v, cache_pool = lax.optimization_barrier(
        (qkv_weight[:, 1], qkv_weight[:, 2], cache_pool) + gate
    )[:3]
    base_k, base_v = gather.base_stages(later_k), gather.base_stages(later_v)
    x = norm_permute(all_tokens, norm_gain, places, blocks)
    length = cache_len[0]
    positions = PPAGES * PAGE + length + jnp.arange(rows, dtype=jnp.int32)
    tables = rotary_tables(positions)
    slots = page_table.shape[1]
    slot_of = jnp.argsort(page_table[0]).astype(jnp.int32)
    token_at = slot_of[:, None] * PAGE + jnp.arange(PAGE, dtype=jnp.int32)[None, :]
    bias = jnp.where(token_at < length, 0.0, NEGATIVE).astype(jnp.float32).reshape(1, slots * PAGE)
    cache_k = cache_pool[:, :, 0].reshape(slots * PAGE, width)
    cache_v = cache_pool[:, :, 1].reshape(slots * PAGE, width)

    q = [project(x, q_pieces[s], tables, bool(s), True, True) for s in range(2)]
    pairs = half // LANES
    states = []
    for s in range(2):
        for at in range(pairs):
            if states:
                bias = after(bias, states[-1][2][2])
            state = cache_attention(q[s], cache_k, cache_v, bias, at, s * pairs + at, 1)
            states.append((s, at, state))
    seen = lambda i: states[min(i, len(states) - 1)][2][2]
    base_k, base_v = lax.optimization_barrier((base_k, base_v, q_pieces[0][1], q_pieces[1][1]))[:2]
    first_k = gather.first_stage(base_k, False)
    first_v = gather.first_stage(base_v, True)
    first_k, first_v, later_o, held = lax.optimization_barrier(
        (first_k, first_v, out_weight, prefix_pool, seen(1))
    )[:4]
    k_pieces = (first_k, gather.second_stage(first_k, False))
    v_pieces = (first_v, gather.second_stage(first_v, True))
    oa, ob = halves(later_o)
    oa, ob = gather.base_stages(oa), gather.base_stages(ob)
    shard_rows = prefix_pool.shape[0]
    per_page = PAGE // shard_rows
    page_ids = lax.dynamic_slice_in_dim(group_pages, group_ids[0] * PPAGES, PPAGES)
    need = (page_ids[:, None] * per_page + jnp.arange(per_page, dtype=jnp.int32)[None, :]).reshape(-1)
    need_there = flip(need, "wide", wide, gather.v)
    for bit in gather.order[:-1]:
        if bit == gather.u:
            oa, ob, held = lax.optimization_barrier((oa, ob, held, seen(5)))[:3]
        held = jnp.concatenate([held, flip(held, "wide", wide, bit)], axis=0)

    oa, ob = gather.first_stage(oa, False), gather.first_stage(ob, True)
    oa, ob, held = lax.optimization_barrier((oa, ob, held, seen(7)))[:3]
    o_pieces = ((oa, gather.second_stage(oa, False)), (ob, gather.second_stage(ob, True)))

    def pick(ids):
        relative = ids ^ me
        at = jnp.zeros_like(ids)
        for k, bit in enumerate(gather.order[:-1]):
            at = at + (((relative >> bit) & 1) << k)
        return jnp.concatenate(
            [
                lax.dynamic_slice_in_dim(held, at[i] * shard_rows, shard_rows)
                for i in range(ids.shape[0])
            ],
            axis=0,
        )

    sent = flip(pick(need_there), "wide", wide, gather.v)
    from_there = jnp.repeat(((need ^ me) >> gather.v) & 1, shard_rows)
    prefix = jnp.where(from_there[:, None, None] == 1, sent, pick(need))
    prefix_k, prefix_v = prefix[:, 0], prefix[:, 1]

    k = project(x, k_pieces, tables, False, True, False)
    v = project(x, v_pieces, tables, True, False, False)
    prefix_k, prefix_v = lax.optimization_barrier(
        (prefix_k, prefix_v, o_pieces[0][0], o_pieces[1][0])
    )[:2]
    attended = jnp.concatenate(
        [
            own_attention(q[s], k, v, prefix_k, prefix_v, state, at, s * pairs + at)
            for s, at, state in states
        ],
        axis=1,
    )
    new_pages = jnp.stack([k, v], axis=1)
    all_heads = narrow_gather(attended, narrow)
    branch_out = output(all_heads, places, *o_pieces)
    return (branch_out, new_pages)


def solution(mesh):
    placed = (
        P("wide", "narrow"),
        P(),
        P("wide", None, "narrow"),
        P("wide", "narrow"),
        P("wide", None, None, "narrow"),
        P("wide", None, "narrow"),
        P("wide", None),
        P("wide"),
        P("wide"),
        P(),
    )
    return jax.shard_map(
        functools.partial(local, mesh.shape["wide"], mesh.shape["narrow"]),
        mesh=mesh,
        in_specs=placed,
        out_specs=(P("wide", "narrow"), P("wide", None, "narrow")),
        check_vma=False,
    )
```

```python
import functools

import jax
import jax.numpy as jnp
from jax import lax
from jax.experimental import pallas as pl
from jax.experimental.pallas import tpu as pltpu
from jax.sharding import PartitionSpec as P

HEAD_DIM = 64
ROT = 16
PAGE = 128
PPAGES = 2
LANES = 128
NEGATIVE = -1e30
LOG2E = 1.4426950408889634
VMEM = 44 * 1024 * 1024


def flip(value, axis, size, bit):
    pairs = [(i, i ^ (1 << bit)) for i in range(size)]
    return lax.ppermute(value, axis, pairs)


def after(value, earlier):
    return lax.optimization_barrier((value, earlier))[0]


class Gather:
    def __init__(self, me, size, shard_rows):
        self.me, self.size = me, size
        bits = size.bit_length() - 1
        self.low = max(0, (LANES // shard_rows).bit_length() - 1)
        order = list(range(bits))
        if self.low == 0:
            order = order[2:][::-1] + order[:2]
        self.base, self.u, self.v = order[:-2], order[-2], order[-1]
        self.order = order

    def base_stages(self, piece):
        for k, bit in enumerate(self.base):
            got = flip(piece, "wide", self.size, bit)
            if k < self.low:
                upper = (self.me >> bit) & 1
                piece = jnp.where(
                    upper == 1,
                    jnp.concatenate([got, piece], axis=0),
                    jnp.concatenate([piece, got], axis=0),
                )
            else:
                piece = jnp.concatenate([piece, got], axis=0)
        return piece

    def last_stages(self, piece, swapped):
        first, second = (self.v, self.u) if swapped else (self.u, self.v)
        piece = jnp.concatenate([piece, flip(piece, "wide", self.size, first)], axis=0)
        return piece, flip(piece, "wide", self.size, second)

    def first_stage(self, piece, swapped):
        bit = self.v if swapped else self.u
        return jnp.concatenate([piece, flip(piece, "wide", self.size, bit)], axis=0)

    def second_stage(self, piece, swapped):
        return flip(piece, "wide", self.size, self.u if swapped else self.v)

    def blocks(self):
        relative = [0]
        for bit in self.order[self.low :]:
            relative = relative + [r ^ (1 << (bit - self.low)) for r in relative]
        return jnp.asarray(relative, jnp.int32) ^ (self.me >> self.low)


def norm_body(src_ref, blk_ref, x_ref, gain_ref, out_ref):
    wide_x = x_ref[...].astype(jnp.float32)
    mean = jnp.mean(wide_x, axis=1, keepdims=True)
    centered = wide_x - mean
    inv = lax.rsqrt(jnp.mean(centered * centered, axis=1, keepdims=True) + 1e-05)
    for j in range(x_ref.shape[1] // LANES):
        src = pl.multiple_of(src_ref[j] * LANES, LANES)
        blk = pl.multiple_of(blk_ref[j] * LANES, LANES)
        part = x_ref[:, pl.ds(src, LANES)].astype(jnp.float32) - mean
        out_ref[:, j * LANES : (j + 1) * LANES] = (
            part * inv * gain_ref[:, pl.ds(blk, LANES)]
        ).astype(jnp.bfloat16)


def norm_permute(tokens, gain, src, blk):
    rows, width = tokens.shape
    tile = 256
    return pl.pallas_call(
        norm_body,
        grid_spec=pltpu.PrefetchScalarGridSpec(
            num_scalar_prefetch=2,
            grid=(rows // tile,),
            in_specs=[
                pl.BlockSpec((tile, width), lambda i, s, b: (i, 0)),
                pl.BlockSpec((1, width), lambda i, s, b: (0, 0)),
            ],
            out_specs=pl.BlockSpec((tile, width), lambda i, s, b: (i, 0)),
        ),
        out_shape=jax.ShapeDtypeStruct((rows, width), jnp.bfloat16),
        compiler_params=pltpu.CompilerParams(vmem_limit_bytes=VMEM),
        cost_estimate=pl.CostEstimate(
            flops=10 * rows * width, bytes_accessed=4 * rows * width, transcendentals=0
        ),
    )(src, blk, tokens, gain.reshape(1, width))


def split_dot(x, p_ref, r_ref, swapped):
    quarter = p_ref.shape[0] // 2
    groups = (0, 2, 1, 3) if swapped else (0, 1, 2, 3)

    def one(at, w):
        return jnp.dot(
            x(groups[at] * quarter, quarter), w, preferred_element_type=jnp.float32
        )

    return (
        one(0, p_ref[:quarter]) + one(1, p_ref[quarter:])
    ) + (one(2, r_ref[:quarter]) + one(3, r_ref[quarter:]))


def project_body(swapped, rotate, scale, x_ref, p_ref, r_ref, c_ref, s_ref, t_ref, *outs):
    total = split_dot(lambda at, n: x_ref[:, at : at + n], p_ref, r_ref, swapped)
    parts = []
    for j in range(total.shape[1] // LANES):
        part = total[:, j * LANES : (j + 1) * LANES]
        if rotate:
            part = (
                part * c_ref[...]
                + pltpu.roll(part, LANES - ROT // 2, 1) * s_ref[...]
                + pltpu.roll(part, ROT // 2, 1) * t_ref[...]
            )
        part = part.astype(jnp.bfloat16)
        if scale:
            part = part * jnp.bfloat16(0.125)
        outs[0][:, j * LANES : (j + 1) * LANES] = part


def project(x, pieces, tables, swapped, rotate, scale):
    rows, depth = x.shape
    half, columns = pieces[0].shape
    tile = min(256, columns)
    whole = lambda i: (0, 0)
    col = lambda i: (0, i)
    return pl.pallas_call(
        functools.partial(project_body, swapped, rotate, scale),
        grid=(columns // tile,),
        in_specs=[
            pl.BlockSpec((rows, depth), whole),
            pl.BlockSpec((half, tile), col),
            pl.BlockSpec((half, tile), col),
        ]
        + [pl.BlockSpec((rows, LANES), whole)] * 3,
        out_specs=pl.BlockSpec((rows, tile), col),
        out_shape=jax.ShapeDtypeStruct((rows, columns), jnp.bfloat16),
        compiler_params=pltpu.CompilerParams(vmem_limit_bytes=VMEM),
        cost_estimate=pl.CostEstimate(
            flops=2 * rows * depth * columns,
            bytes_accessed=2 * (rows * depth + depth * columns + rows * columns),
            transcendentals=0,
        ),
    )(x, *pieces, *tables)


def head_of(pair, head):
    lane = lax.broadcasted_iota(jnp.int32, pair.shape, 1)
    mine = (lane >= HEAD_DIM) if head else (lane < HEAD_DIM)
    return jnp.where(mine, pair, jnp.zeros_like(pair))


def scores_of(q, k):
    return lax.dot_general(q, k, (((1,), (1,)), ((), ())), preferred_element_type=jnp.float32)


def soft(q_ref, k, v, bias, valid):
    ones = jnp.ones_like(v)
    v_ones = jnp.concatenate([v, ones], axis=1)
    rows = q_ref.shape[0]
    found = []
    for head in range(2):
        s = scores_of(head_of(q_ref[...], head), k)
        if bias is not None:
            s = s + bias
        if valid is not None:
            s = jnp.where(valid, s, NEGATIVE)
        m = jnp.max(s, axis=1, keepdims=True)
        p = jnp.exp2((s - m) * LOG2E).astype(jnp.bfloat16)
        o = jnp.dot(p, v_ones, preferred_element_type=jnp.float32)
        found.append((o[:, :LANES], o[:, LANES:], jnp.broadcast_to(m, (rows, LANES))))
    lane = lax.broadcasted_iota(jnp.int32, (rows, LANES), 1) < HEAD_DIM
    return [jnp.where(lane, a, b) for a, b in zip(*found)]


def cache_body(q_ref, k_ref, v_ref, bias_ref, o_ref, l_ref, m_ref):
    o, l, m = soft(q_ref, k_ref[...], v_ref[...], bias_ref[...], None)
    o_ref[...] = o
    l_ref[...] = l
    m_ref[...] = m


def cache_attention(q, k, v, bias, q_at, kv_at, pairs):
    rows = q.shape[0]
    keys = k.shape[0]
    tile = 256
    shape = jax.ShapeDtypeStruct((rows, pairs * LANES), jnp.float32)
    out = pl.BlockSpec((tile, LANES), lambda h, i: (i, h))
    kv = pl.BlockSpec((keys, LANES), lambda h, i: (0, h + kv_at))
    return pl.pallas_call(
        cache_body,
        grid=(pairs, rows // tile),
        in_specs=[
            pl.BlockSpec((tile, LANES), lambda h, i: (i, h + q_at)),
            kv,
            kv,
            pl.BlockSpec((1, keys), lambda h, i: (0, 0)),
        ],
        out_specs=[out] * 3,
        out_shape=[shape] * 3,
        compiler_params=pltpu.CompilerParams(vmem_limit_bytes=VMEM),
        cost_estimate=pl.CostEstimate(flops=1000, bytes_accessed=1000, transcendentals=0),
    )(q, k, v, bias)


def own_body(q_ref, kn_ref, vn_ref, kp_ref, vp_ref, o_ref, l_ref, m_ref, out_ref):
    rows = q_ref.shape[0]
    shared = kp_ref.shape[0]
    keys = shared + kn_ref.shape[0]
    k = jnp.concatenate([kp_ref[...], kn_ref[...]], axis=0)
    v = jnp.concatenate([vp_ref[...], vn_ref[...]], axis=0)
    query = pl.program_id(1) * rows + lax.broadcasted_iota(jnp.int32, (rows, keys), 0)
    key = lax.broadcasted_iota(jnp.int32, (rows, keys), 1) - shared
    o2, l2, m2 = soft(q_ref, k, v, None, key <= query)
    m1 = m_ref[...]
    m = jnp.maximum(m1, m2)
    f1 = jnp.exp2((m1 - m) * LOG2E)
    f2 = jnp.exp2((m2 - m) * LOG2E)
    out_ref[...] = (
        (o_ref[...] * f1 + o2 * f2) / (l_ref[...] * f1 + l2 * f2)
    ).astype(jnp.bfloat16)


def own_attention(q, kn, vn, kp, vp, state, q_at, kv_at):
    rows = q.shape[0]
    shared = kp.shape[0]
    pairs = state[0].shape[1] // LANES
    tile = 256
    here = pl.BlockSpec((tile, LANES), lambda h, i: (i, h))
    new = pl.BlockSpec((rows, LANES), lambda h, i: (0, h + kv_at))
    pre = pl.BlockSpec((shared, LANES), lambda h, i: (0, h + kv_at))
    return pl.pallas_call(
        own_body,
        grid=(pairs, rows // tile),
        in_specs=[
            pl.BlockSpec((tile, LANES), lambda h, i: (i, h + q_at)),
            new,
            new,
            pre,
            pre,
            here,
            here,
            here,
        ],
        out_specs=here,
        out_shape=jax.ShapeDtypeStruct((rows, pairs * LANES), jnp.bfloat16),
        compiler_params=pltpu.CompilerParams(vmem_limit_bytes=VMEM),
        cost_estimate=pl.CostEstimate(flops=1000, bytes_accessed=1000, transcendentals=0),
    )(q, kn, vn, kp, vp, *state)


def output_body(src_ref, x_ref, pa_ref, ra_ref, pb_ref, rb_ref, out_ref, turned):
    for j in range(x_ref.shape[1] // LANES):
        src = pl.multiple_of(src_ref[j] * LANES, LANES)
        turned[:, j * LANES : (j + 1) * LANES] = x_ref[:, pl.ds(src, LANES)]
    half = pa_ref.shape[1]
    x = lambda at, n: turned[:, at : at + n]
    out_ref[:, :half] = split_dot(x, pa_ref, ra_ref, False).astype(jnp.bfloat16)
    out_ref[:, half:] = split_dot(x, pb_ref, rb_ref, True).astype(jnp.bfloat16)


def output(x, src, pieces_a, pieces_b):
    rows, depth = x.shape
    half, columns = pieces_a[0].shape
    tile = 256
    weight = pl.BlockSpec((half, columns), lambda i, s: (0, 0))
    return pl.pallas_call(
        output_body,
        grid_spec=pltpu.PrefetchScalarGridSpec(
            num_scalar_prefetch=1,
            grid=(rows // tile,),
            in_specs=[pl.BlockSpec((tile, depth), lambda i, s: (i, 0))] + [weight] * 4,
            out_specs=pl.BlockSpec((tile, 2 * columns), lambda i, s: (i, 0)),
            scratch_shapes=[pltpu.VMEM((tile, depth), jnp.bfloat16)],
        ),
        out_shape=jax.ShapeDtypeStruct((rows, 2 * columns), jnp.bfloat16),
        compiler_params=pltpu.CompilerParams(vmem_limit_bytes=VMEM),
        cost_estimate=pl.CostEstimate(
            flops=4 * rows * depth * columns,
            bytes_accessed=2 * depth * (rows + 2 * columns),
            transcendentals=0,
        ),
    )(src, x, *pieces_a, *pieces_b)


def rotary_tables(positions):
    half_rot = ROT // 2
    frequency = 10000.0 ** (-(jnp.arange(half_rot, dtype=jnp.float32) * 2.0 / ROT))
    angles = positions.astype(jnp.float32)[:, None] * frequency[None, :]
    cos, sin = jnp.cos(angles), jnp.sin(angles)
    rows = positions.shape[0]
    rest = jnp.zeros((rows, HEAD_DIM - ROT), jnp.float32)
    none = jnp.zeros_like(sin)
    tables = (
        jnp.concatenate([cos, cos, rest + 1.0], axis=1),
        jnp.concatenate([-sin, none, rest], axis=1),
        jnp.concatenate([none, sin, rest], axis=1),
    )
    return [jnp.concatenate([t, t], axis=1) for t in tables]


def narrow_gather(value, size):
    bit = 0
    while (1 << bit) < size:
        value = jnp.concatenate([value, flip(value, "narrow", size, bit)], axis=1)
        bit += 1
    return value


def local(
    wide,
    narrow,
    tokens,
    norm_gain,
    qkv_weight,
    out_weight,
    cache_pool,
    prefix_pool,
    page_table,
    cache_len,
    group_ids,
    group_pages,
):
    rows = tokens.shape[0]
    width = qkv_weight.shape[2]
    half = width // 2
    me = lax.axis_index("wide")
    me_narrow = lax.axis_index("narrow")
    shard = qkv_weight.shape[0]
    gather = Gather(me, wide, shard)
    per_narrow = width // LANES
    blocks = gather.blocks()
    places = ((blocks // per_narrow) ^ me_narrow) * per_narrow + blocks % per_narrow

    all_tokens = narrow_gather(tokens, narrow)

    def halves(w):
        return w[:, :half], w[:, half:]

    qa, qb = halves(qkv_weight[:, 0])
    qa, qb = gather.base_stages(qa), gather.base_stages(qb)
    q_pieces = (gather.last_stages(qa, False), gather.last_stages(qb, True))
    gate = (q_pieces[0][0], q_pieces[1][0])
    later_k, later_v, cache_pool = lax.optimization_barrier(
        (qkv_weight[:, 1], qkv_weight[:, 2], cache_pool) + gate
    )[:3]
    base_k, base_v = gather.base_stages(later_k), gather.base_stages(later_v)
    x = norm_permute(all_tokens, norm_gain, places, blocks)
    length = cache_len[0]
    positions = PPAGES * PAGE + length + jnp.arange(rows, dtype=jnp.int32)
    tables = rotary_tables(positions)
    slots = page_table.shape[1]
    slot_of = jnp.argsort(page_table[0]).astype(jnp.int32)
    token_at = slot_of[:, None] * PAGE + jnp.arange(PAGE, dtype=jnp.int32)[None, :]
    bias = jnp.where(token_at < length, 0.0, NEGATIVE).astype(jnp.float32).reshape(1, slots * PAGE)
    cache_k = cache_pool[:, :, 0].reshape(slots * PAGE, width)
    cache_v = cache_pool[:, :, 1].reshape(slots * PAGE, width)

    q = [project(x, q_pieces[s], tables, bool(s), True, True) for s in range(2)]
    pairs = half // LANES
    base_k, base_v = lax.optimization_barrier((base_k, base_v, q_pieces[0][1], q_pieces[1][1]))[:2]
    first_k = gather.first_stage(base_k, False)
    first_v = gather.first_stage(base_v, True)
    states = []
    seen = lambda i: states[min(i, len(states) - 1)][2][2]
    last = 2 * pairs - 1
    for s in range(2):
        for at in range(pairs):
            if states:
                bias = after(bias, states[-1][2][2])
            if len(states) == min(2, last):
                first_k, first_v = lax.optimization_barrier((first_k, first_v, seen(1)))[:2]
                k_pieces = (first_k, gather.second_stage(first_k, False))
                v_pieces = (first_v, gather.second_stage(first_v, True))
            if len(states) == min(6, last):
                bias = lax.optimization_barrier((bias, k_pieces[1], v_pieces[1]))[0]
            state = cache_attention(q[s], cache_k, cache_v, bias, at, s * pairs + at, 1)
            states.append((s, at, state))
    later_o, held = lax.optimization_barrier((out_weight, prefix_pool, seen(3)))[:2]
    oa, ob = halves(later_o)
    oa, ob = gather.base_stages(oa), gather.base_stages(ob)
    shard_rows = prefix_pool.shape[0]
    per_page = PAGE // shard_rows
    page_ids = lax.dynamic_slice_in_dim(group_pages, group_ids[0] * PPAGES, PPAGES)
    need = (page_ids[:, None] * per_page + jnp.arange(per_page, dtype=jnp.int32)[None, :]).reshape(-1)
    need_there = flip(need, "wide", wide, gather.v)
    for bit in gather.order[:-1]:
        if bit == gather.u:
            oa, ob, held = lax.optimization_barrier((oa, ob, held, seen(5), k_pieces[1], v_pieces[1]))[:3]
        held = jnp.concatenate([held, flip(held, "wide", wide, bit)], axis=0)

    oa, ob = gather.first_stage(oa, False), gather.first_stage(ob, True)
    oa, ob, held = lax.optimization_barrier((oa, ob, held, seen(7)))[:3]
    o_pieces = ((oa, gather.second_stage(oa, False)), (ob, gather.second_stage(ob, True)))

    def pick(ids):
        relative = ids ^ me
        at = jnp.zeros_like(ids)
        for k, bit in enumerate(gather.order[:-1]):
            at = at + (((relative >> bit) & 1) << k)
        return jnp.concatenate(
            [
                lax.dynamic_slice_in_dim(held, at[i] * shard_rows, shard_rows)
                for i in range(ids.shape[0])
            ],
            axis=0,
        )

    sent = flip(pick(need_there), "wide", wide, gather.v)
    from_there = jnp.repeat(((need ^ me) >> gather.v) & 1, shard_rows)
    prefix = jnp.where(from_there[:, None, None] == 1, sent, pick(need))
    prefix_k, prefix_v = prefix[:, 0], prefix[:, 1]

    k = project(x, k_pieces, tables, False, True, False)
    v = project(x, v_pieces, tables, True, False, False)
    prefix_k, prefix_v = lax.optimization_barrier(
        (prefix_k, prefix_v, o_pieces[0][0], o_pieces[1][0])
    )[:2]
    late_k, late_v = lax.optimization_barrier(
        (prefix_k, prefix_v, o_pieces[0][1], o_pieces[1][1])
    )[:2]
    shared = ((prefix_k, prefix_v), (late_k, late_v))
    attended = jnp.concatenate(
        [
            own_attention(q[s], k, v, *shared[s], state, at, s * pairs + at)
            for s, at, state in states
        ],
        axis=1,
    )
    new_pages = jnp.stack([k, v], axis=1)
    all_heads = narrow_gather(attended, narrow)
    branch_out = output(all_heads, places, *o_pieces)
    return (branch_out, new_pages)


def solution(mesh):
    placed = (
        P("wide", "narrow"),
        P(),
        P("wide", None, "narrow"),
        P("wide", "narrow"),
        P("wide", None, None, "narrow"),
        P("wide", None, "narrow"),
        P("wide", None),
        P("wide"),
        P("wide"),
        P(),
    )
    return jax.shard_map(
        functools.partial(local, mesh.shape["wide"], mesh.shape["narrow"]),
        mesh=mesh,
        in_specs=placed,
        out_specs=(P("wide", "narrow"), P("wide", None, "narrow")),
        check_vma=False,
    )
```
